1024 devices in a mesh: pair: 64 (over x, z), virt: 16 (over y, core).
Axes of the slice: x: 4, y: 8, z: 16, core: 2. Of those that a mesh axis runs over, the one named last changes fastest.
Arguments:
- amps: bfloat16 [128, 4096, 512], P('pair', 'virt'), may hold values from -6 to 6
- fock: bfloat16 [4096, 4096], P('virt'), may hold values from -0.15625 to 0.15625
- ladder: bfloat16 [4096, 4096], P('virt'), may hold values from -0.15625 to 0.15625
- couple: bfloat16 [512, 512], replicated, may hold values from -0.25 to 0.25
- tile_list: int32 [128, 32, 12], P('pair', 'virt'), may hold values from 0 to 31, as said below
Outputs:
- residual: bfloat16 [128, 4096, 512], P('pair', 'virt')
The draws below stay inside these ranges and needn't reach their ends.
Inputs may be any that keep to these rules, and one draw needn't show every extreme that they name: `tile_list`: within one row of the last dimension the 12 tiles are distinct.
All inputs are finite; a program needn't handle non-finite values.
Results may differ from the reference program's by a relative error of at most 0.0053.
Values may be sent and summed in bfloat16 or wider, within the bound.
No kernel may reach another device: no remote copies, remote signals or barrier semaphores. Data moves between devices by JAX's collectives and lax.ppermute only.
A program may use at most 64 MiB of HBM per device.

```python
import jax
import jax.numpy as jnp
import numpy as np
from jax import lax

TILE = 128
TILES = 32
NNZ = 12
PAIRS_DEV = 2
NV = 4096
NB = 512
NPAIR = 128
N_PAIR = 64


def draw_tile_list(key, part):
    key = jax.random.fold_in(key, 7)
    scores = jax.random.randint(key, (NPAIR, TILES, TILES), 0, 1 << 20, dtype=jnp.int32)
    scores = scores * TILES + jnp.arange(TILES, dtype=jnp.int32)
    ranked = jnp.argsort(scores, axis=-1)
    return ranked[..., :NNZ].astype(jnp.int32)


def levels(rng, shape, cuts, least, high):
    gain, own = 1.0, jax.random.fold_in(rng, 6)
    for axis_at, shards_of in cuts:
        draws = jnp.exp(jax.random.uniform(jax.random.fold_in(own, axis_at), (shards_of,), jnp.float32, least / len(cuts), high / len(cuts)))
        gain = gain * jnp.repeat(draws, shape[axis_at] // shards_of).reshape([-1 if axis == axis_at else 1 for axis in range(len(shape))])
    return gain


def centred(rng, extent, spread, bound, cuts=(), kind=jnp.bfloat16):
    values = spread * jax.random.normal(rng, extent, jnp.float32)
    if cuts:
        values = values * levels(rng, extent, cuts, -0.22, 0.18)
    return jnp.clip(values, -bound, bound).astype(kind)


def setup_inputs(seed: int = 0) -> dict:
    splits = jax.random.split(jax.random.key(seed), 6)
    amps = centred(splits[0], (NPAIR, NV, NB), 1.0, 6.0, ((0, 64), (1, 16)))
    fock = centred(splits[1], (NV, NV), (NNZ * TILE) ** -0.5, 0.15625, ((0, 16),))
    ladder = centred(splits[2], (NV, NV), (NNZ * TILE) ** -0.5, 0.15625, ((0, 16),))
    couple = centred(splits[3], (NB, NB), NB ** -0.5, 0.25)
    tile_list = draw_tile_list(jax.random.fold_in(splits[5], 71), 0)
    return dict(amps=amps, fock=fock, ladder=ladder, couple=couple, tile_list=tile_list)


def reverse_bits(count):
    nbits = count.bit_length() - 1
    result = []
    for value in range(count):
        flipped = 0
        for position in range(nbits):
            flipped = flipped | (((value >> position) & 1) << (nbits - 1 - position))
        result.append(count - 1 - flipped)
    return np.array(result, dtype=np.int32)


def reference(amps, fock, ladder, couple, tile_list):
    fock_tiles = fock.reshape(TILES, TILE, TILES, TILE).transpose(0, 2, 1, 3)
    ladder_tiles = ladder.reshape(TILES, TILE, TILES, TILE).transpose(0, 2, 1, 3)
    rows_idx = jnp.arange(TILES, dtype=jnp.int32)[:, None]

    def per_pair(operands):
        amp_pair, listed = operands
        amp_tiles = amp_pair.reshape(TILES, TILE, NB)
        amp_sel = amp_tiles[listed].astype(jnp.float32)
        fock_sel = fock_tiles[rows_idx, listed].astype(jnp.float32)
        ladder_sel = ladder_tiles[rows_idx, listed].astype(jnp.float32)
        cycle = jnp.einsum("kzxy,kzyb->kxb", fock_sel, amp_sel).reshape(NV, NB)
        lad = jnp.einsum("kzxy,kzyb->kxb", ladder_sel, amp_sel).reshape(NV, NB).astype(jnp.bfloat16)
        inner = jnp.dot(lad, couple, preferred_element_type=jnp.float32)
        return (cycle + inner).astype(jnp.bfloat16)

    halves = lax.map(per_pair, (amps, tile_list))
    mirror_dev = reverse_bits(N_PAIR)
    mirror_pair = (mirror_dev[:, None] * PAIRS_DEV + np.arange(PAIRS_DEV, dtype=np.int32)[None, :]).reshape(-1)
    mirrored = halves[jnp.asarray(mirror_pair, dtype=jnp.int32)]
    return (halves.astype(jnp.float32) + mirrored.astype(jnp.float32)).astype(jnp.bfloat16)
```

```python
import functools

import jax
import jax.numpy as jnp
from jax import lax
from jax.experimental import pallas as pl
from jax.experimental.pallas import tpu as pltpu
from jax.sharding import PartitionSpec as P

TILE = 128
HALF = 256
EXTRA = 16
SLOTS = 8
GROUP = 4


def core_swap(block):
    count = lax.axis_size("virt")
    return lax.ppermute(block, "virt", [(v, v ^ 1) for v in range(count)])


def ring_step(block):
    chips = lax.axis_size("virt") // 2
    route = [(2 * c, 2 * ((c + 1) % chips)) for c in range(chips)]
    route += [(2 * c + 1, 2 * ((c - 1) % chips) + 1) for c in range(chips)]
    return lax.ppermute(block, "virt", route)


def mirror_swap(block):
    count = lax.axis_size("pair")
    nbits = count.bit_length() - 1
    route = []
    for low in range(count):
        flipped = sum(((low >> b) & 1) << (nbits - 1 - b) for b in range(nbits))
        route.append((low, count - 1 - flipped))
    return lax.ppermute(block, "pair", route)


def message(amp_pair, listed):
    flat = listed.reshape(1, -1).astype(amp_pair.dtype)
    tail = jnp.pad(flat, ((0, EXTRA - 1), (0, amp_pair.shape[1] - flat.shape[1])))
    return jnp.concatenate([amp_pair, tail], axis=0)


def lists_of(msg, nnz):
    rows = HALF // TILE
    return msg[HALF, : rows * nnz].astype(jnp.int32).reshape(rows, nnz)


def gather_halves(own, other):
    slots = [own]
    x, s = own, other
    for _ in range(3):
        x, s = ring_step(x), ring_step(s)
        slots += [x, s]
    slots.append(ring_step(x))
    return slots


def part_kernel(units, slot_ref, mask_ref, *refs):
    a_refs = refs[: units * SLOTS]
    f_refs = refs[units * SLOTS : units * SLOTS + 4]
    couple_hbm = refs[units * SLOTS + 4]
    own_ref, sib_ref = refs[units * SLOTS + 5 : units * SLOTS + 7]
    a_buf, f_buf, m_buf, acc, couple_buf, a_sem, f_sem, c_sem = refs[units * SLOTS + 7 :]

    def f_copy(i, s):
        col = pl.multiple_of(slot_ref[s] * TILE, HALF)
        return pltpu.make_async_copy(f_refs[i].at[:, pl.ds(col, HALF)], f_buf.at[i, s], f_sem.at[i, s])

    def a_copy(u, s):
        return pltpu.make_async_copy(
            a_refs[u * SLOTS + s].at[pl.ds(0, HALF)], a_buf.at[u, pl.ds(HALF * s, HALF)], a_sem.at[u, s]
        )

    c_copy = pltpu.make_async_copy(couple_hbm, couple_buf, c_sem)
    for s in range(SLOTS):
        for i in range(4):
            f_copy(i, s).start()
        a_copy(0, s).start()
    for u in range(1, units):
        for s in range(SLOTS):
            a_copy(u, s).start()
    c_copy.start()
    for u in range(units):
        for g in range(SLOTS // GROUP):
            for sg in range(GROUP):
                s = g * GROUP + sg
                if u == 0:
                    for i in range(4):
                        f_copy(i, s).wait()
                a_copy(u, s).wait()
                for i in range(4):
                    for rt in range(2):
                        for q in range(2):
                            keep = mask_ref[u * 4 + (i % 2) * 2 + rt, slot_ref[s] + q] != 0
                            tile = f_buf[i, s, rt * TILE : (rt + 1) * TILE, q * TILE : (q + 1) * TILE]
                            m_buf[
                                i * HALF + rt * TILE : i * HALF + (rt + 1) * TILE,
                                sg * HALF + q * TILE : sg * HALF + (q + 1) * TILE,
                            ] = jnp.where(keep, tile, jnp.zeros_like(tile))
            prod = jnp.dot(
                m_buf[...],
                a_buf[u, g * GROUP * HALF : (g + 1) * GROUP * HALF, :],
                preferred_element_type=jnp.float32,
            )
            if u == 0 and g == 0:
                acc[...] = prod
            else:
                acc[...] += prod
    c_copy.wait()
    lad = acc[2 * HALF :, :].astype(jnp.bfloat16)
    total = acc[: 2 * HALF, :] + jnp.dot(lad, couple_buf[...], preferred_element_type=jnp.float32)
    own_ref[...] = total[:HALF, :]
    sib_ref[...] = total[HALF:, :]


def partial_sums(slot_tiles, masks, unit_slots, mats, couple):
    units = len(unit_slots)
    width = couple.shape[0]
    flat = [block for slots in unit_slots for block in slots]
    smem = pl.BlockSpec(memory_space=pltpu.SMEM)
    anywhere = pl.BlockSpec(memory_space=pl.ANY)
    vmem = pl.BlockSpec(memory_space=pltpu.VMEM)
    flops = 2 * units * 4 * HALF * SLOTS * HALF * width + 2 * 2 * HALF * width * width
    return pl.pallas_call(
        functools.partial(part_kernel, units),
        out_shape=[jax.ShapeDtypeStruct((HALF, width), jnp.float32)] * 2,
        in_specs=[smem, smem] + [anywhere] * (len(flat) + 5),
        out_specs=[vmem, vmem],
        scratch_shapes=[
            pltpu.VMEM((units, SLOTS * HALF, width), jnp.bfloat16),
            pltpu.VMEM((4, SLOTS, HALF, HALF), jnp.bfloat16),
            pltpu.VMEM((4 * HALF, GROUP * HALF), jnp.bfloat16),
            pltpu.VMEM((4 * HALF, width), jnp.float32),
            pltpu.VMEM((width, width), jnp.bfloat16),
            pltpu.SemaphoreType.DMA((units, SLOTS)),
            pltpu.SemaphoreType.DMA((4, SLOTS)),
            pltpu.SemaphoreType.DMA,
        ],
        compiler_params=pltpu.CompilerParams(vmem_limit_bytes=36 * 1024 * 1024),
        cost_estimate=pl.CostEstimate(flops=flops, bytes_accessed=8 << 20, transcendentals=0),
        name="partial_sums",
    )(slot_tiles, masks, *flat, *mats, couple)


def per_device(amps, fock, ladder, couple, tile_list):
    chips = lax.axis_size("virt") // 2
    per_chip = 2 * HALF // TILE
    total_tiles = fock.shape[1] // TILE
    nnz = tile_list.shape[2]
    place = lax.axis_index("virt")
    chip, core = place // 2, place % 2
    way = jnp.where(core == 0, -1, 1)

    def slot_tile(hops, other):
        half = jnp.where(other, 1 - core, core)
        return ((chip + way * hops + chips) % chips) * per_chip + half * (HALF // TILE)

    slot_tiles = jnp.stack(
        [slot_tile(h, o) for h, o in ((0, 0), (1, 0), (1, 1), (2, 0), (2, 1), (3, 0), (3, 1), (4, 0))]
    ).astype(jnp.int32)
    columns = jnp.arange(total_tiles, dtype=jnp.int32)

    def mask_of(own_msg, other_msg):
        listed = jnp.concatenate([lists_of(own_msg, nnz), lists_of(other_msg, nnz)], axis=0)
        return jnp.any(listed[:, :, None] == columns, axis=1).astype(jnp.int32)

    msg0 = message(amps[0], tile_list[0])
    msg1 = message(amps[1], tile_list[1])
    far0 = mirror_swap(msg0)
    msg1_other = core_swap(msg1)
    slots1 = gather_halves(msg1, msg1_other)
    mats = (fock, core_swap(fock), ladder, core_swap(ladder))

    own1, sib1 = partial_sums(slot_tiles, mask_of(msg1, msg1_other), [slots1], mats, couple)
    half1 = (own1 + core_swap(sib1)).astype(jnp.bfloat16)
    half1_far = mirror_swap(half1)

    msg0_other = core_swap(msg0)
    far0_other = core_swap(far0)
    slots0 = gather_halves(msg0, msg0_other)
    slots_far = gather_halves(far0, far0_other)
    masks = jnp.concatenate([mask_of(msg0, msg0_other), mask_of(far0, far0_other)], axis=0)
    own0, sib0 = partial_sums(slot_tiles, masks, [slots0, slots_far], mats, couple)
    res0 = (own0 + core_swap(sib0)).astype(jnp.bfloat16)
    res1 = (half1.astype(jnp.float32) + half1_far.astype(jnp.float32)).astype(jnp.bfloat16)
    return jnp.stack([res0, res1])


def solution(mesh):
    in_specs = (
        P("pair", "virt", None),
        P("virt", None),
        P("virt", None),
        P(),
        P("pair", "virt", None),
    )
    out_specs = P("pair", "virt", None)
    return jax.shard_map(
        per_device, mesh=mesh, in_specs=in_specs, out_specs=out_specs, check_vma=False
    )
```

```python
import functools

import jax
import jax.numpy as jnp
from jax import lax
from jax.experimental import pallas as pl
from jax.experimental.pallas import tpu as pltpu
from jax.sharding import PartitionSpec as P

TILE = 128
HALF = 256
EXTRA = 16
VMEM_LIMIT = 24 * 1024 * 1024


def core_swap(block):
    count = lax.axis_size("virt")
    return lax.ppermute(block, "virt", [(v, v ^ 1) for v in range(count)])


def ring_step(block):
    chips = lax.axis_size("virt") // 2
    route = [(2 * c, 2 * ((c + 1) % chips)) for c in range(chips)]
    route += [(2 * c + 1, 2 * ((c - 1) % chips) + 1) for c in range(chips)]
    return lax.ppermute(block, "virt", route)


def mirror_swap(block):
    count = lax.axis_size("pair")
    nbits = count.bit_length() - 1
    route = []
    for low in range(count):
        flipped = sum(((low >> b) & 1) << (nbits - 1 - b) for b in range(nbits))
        route.append((low, count - 1 - flipped))
    return lax.ppermute(block, "pair", route)


def message(amp_pairs, listed):
    pairs, rows, width = amp_pairs.shape
    flat = listed.reshape(pairs, -1).astype(amp_pairs.dtype)
    tail = jnp.pad(flat, ((0, EXTRA - pairs), (0, width - flat.shape[1])))
    return jnp.concatenate([amp_pairs.reshape(pairs * rows, width), tail], axis=0)


def masks_of(own_msg, other_msg, pairs, nnz, total_tiles):
    start, rows = pairs * HALF, HALF // TILE
    lists = [m[start : start + pairs, : rows * nnz].reshape(pairs, rows, nnz) for m in (own_msg, other_msg)]
    listed = jnp.concatenate(lists, axis=1).astype(jnp.int32).reshape(pairs * 2 * rows, nnz)
    columns = jnp.arange(total_tiles, dtype=jnp.int32)
    return jnp.any(listed[:, :, None] == columns, axis=1).astype(jnp.int32)


def after(block, *earlier):
    return lax.optimization_barrier((block, *earlier))[0]


def add_kernel(slots, pairs, has_acc, last, slot_ref, mask_ref, *refs):
    count = len(slots)
    refs = list(refs)
    a_refs = [refs.pop(0) for _ in range(count)]
    f_refs = [refs.pop(0) for _ in range(4)]
    couple_ref = refs.pop(0) if last else None
    acc_in = refs.pop(0) if has_acc else None
    outs = [refs.pop(0) for _ in range(2 if last else 1)]
    m_buf, a_buf = refs[:2]
    depth = count * HALF
    for p in range(pairs):
        for n, slot in enumerate(slots):
            a_buf[n * HALF : (n + 1) * HALF, :] = a_refs[n][p * HALF : (p + 1) * HALF, :]
            for q in range(HALF // TILE):
                tile = slot_ref[slot] + q
                col = pl.multiple_of(tile * TILE, TILE)
                for i in range(4):
                    for rt in range(HALF // TILE):
                        keep = mask_ref[p * 4 + (i % 2) * 2 + rt, tile] != 0
                        block = f_refs[i][rt * TILE : (rt + 1) * TILE, pl.ds(col, TILE)]
                        m_buf[
                            i * HALF + rt * TILE : i * HALF + (rt + 1) * TILE,
                            n * HALF + q * TILE : n * HALF + (q + 1) * TILE,
                        ] = jnp.where(keep, block, jnp.zeros_like(block))
        acc = jnp.dot(m_buf[:, :depth], a_buf[:depth, :], preferred_element_type=jnp.float32)
        if has_acc:
            acc = acc_in[p] + acc
        if last:
            lad = acc[2 * HALF :, :].astype(jnp.bfloat16)
            total = acc[: 2 * HALF, :] + jnp.dot(lad, couple_ref[...], preferred_element_type=jnp.float32)
            outs[0][p] = total[:HALF, :]
            outs[1][p] = total[HALF:, :]
        else:
            outs[0][p] = acc


def add_slots(name, slot_tiles, masks, blocks, slots, pairs, mats, acc=None, couple=None):
    width = blocks[0].shape[1]
    last = couple is not None
    smem = pl.BlockSpec(memory_space=pltpu.SMEM)
    vmem = pl.BlockSpec(memory_space=pltpu.VMEM)
    operands = [*blocks, *mats] + ([couple] if last else []) + ([acc] if acc is not None else [])
    wide = jax.ShapeDtypeStruct((pairs, 4 * HALF, width), jnp.float32)
    half = jax.ShapeDtypeStruct((pairs, HALF, width), jnp.float32)
    flops = 2 * pairs * (4 * HALF * len(slots) * HALF * width + (2 * HALF * width * width if last else 0))
    return pl.pallas_call(
        functools.partial(add_kernel, slots, pairs, acc is not None, last),
        out_shape=[half, half] if last else [wide],
        in_specs=[smem, smem] + [vmem] * len(operands),
        out_specs=[vmem] * (2 if last else 1),
        scratch_shapes=[
            pltpu.VMEM((4 * HALF, len(slots) * HALF), jnp.bfloat16),
            pltpu.VMEM((len(slots) * HALF, width), jnp.bfloat16),
        ],
        compiler_params=pltpu.CompilerParams(vmem_limit_bytes=VMEM_LIMIT),
        cost_estimate=pl.CostEstimate(flops=flops, bytes_accessed=1 << 20, transcendentals=0),
        name=name,
    )(slot_tiles, masks, *operands)


def per_device(amps, fock, ladder, couple, tile_list):
    chips = lax.axis_size("virt") // 2
    per_chip = 2 * HALF // TILE
    total_tiles = fock.shape[1] // TILE
    pairs, _, nnz = tile_list.shape
    place = lax.axis_index("virt")
    chip, core = place // 2, place % 2
    way = jnp.where(core == 0, -1, 1)

    hops = jnp.array([0, 1, 1, 2, 2, 3, 3, 4], dtype=jnp.int32)
    other = jnp.array([0, 0, 1, 0, 1, 0, 1, 0], dtype=jnp.int32)
    half_of = jnp.where(other == 1, 1 - core, core)
    slot_tiles = ((chip + way * hops + chips) % chips * per_chip + half_of * (HALF // TILE)).astype(jnp.int32)

    x0 = message(amps, tile_list)
    s0 = core_swap(x0)
    mats = (fock, core_swap(after(fock, s0)), ladder, core_swap(after(ladder, s0)))
    masks = masks_of(x0, s0, pairs, nnz, total_tiles)
    add = functools.partial(add_slots, slot_tiles=slot_tiles, masks=masks, pairs=pairs, mats=mats)

    x1, s1 = ring_step(x0), ring_step(s0)
    x2, s2 = ring_step(x1), ring_step(s1)
    x3, s3 = ring_step(x2), ring_step(s2)
    (part,) = add("first_slots", blocks=[x0, x1, s1, x2], slots=(0, 1, 2, 3))
    x4 = ring_step(after(x3, part))
    (part,) = add("next_slots", blocks=[s2, x3], slots=(4, 5), acc=part)
    own, sib = add("last_slots", blocks=[s3, x4], slots=(6, 7), acc=part, couple=couple)
    half_term = (own + core_swap(sib)).astype(jnp.bfloat16)
    mirrored = mirror_swap(half_term)
    return (half_term.astype(jnp.float32) + mirrored.astype(jnp.float32)).astype(jnp.bfloat16)


def solution(mesh):
    in_specs = (
        P("pair", "virt", None),
        P("virt", None),
        P("virt", None),
        P(),
        P("pair", "virt", None),
    )
    out_specs = P("pair", "virt", None)
    return jax.shard_map(
        per_device, mesh=mesh, in_specs=in_specs, out_specs=out_specs, check_vma=False
    )
```

```python
import functools

import jax
import jax.numpy as jnp
from jax import lax
from jax.experimental import pallas as pl
from jax.experimental.pallas import tpu as pltpu
from jax.sharding import PartitionSpec as P

TILE = 128
HALF = 256
SPLIT = HALF // TILE
VMEM_LIMIT = 24 * 1024 * 1024
HOPS = (None, (0, 0), (1, 0), (1, 1), (2, 0), (2, 1), (3, 0), (3, 1), (4, 0))
ORDER = (1, 2, 3, -1, -2, -3, 4, 5, -4, -5, 6, -6, -7, 7, 8, -8)


def core_swap(block):
    count = lax.axis_size("virt")
    return lax.ppermute(block, "virt", [(v, v ^ 1) for v in range(count)])


def ring_step(block, cross=0):
    chips = lax.axis_size("virt") // 2
    route = [(2 * c + cross, 2 * ((c + 1) % chips)) for c in range(chips)]
    route += [(2 * c + 1 - cross, 2 * ((c - 1) % chips) + 1) for c in range(chips)]
    return lax.ppermute(block, "virt", route)


def mirror_swap(block):
    count = lax.axis_size("pair")
    nbits = count.bit_length() - 1
    route = []
    for low in range(count):
        flipped = sum(((low >> b) & 1) << (nbits - 1 - b) for b in range(nbits))
        route.append((low, count - 1 - flipped))
    return lax.ppermute(block, "pair", route)


def after(block, *earlier):
    return lax.optimization_barrier((block, *earlier))[0]


def screen_kernel(pairs, slot_ref, mask_ref, fock, ladder, out_ref, buf, sem):
    count = buf.shape[1]

    def copies(n):
        col = pl.multiple_of(slot_ref[n] * TILE, HALF)
        return [
            pltpu.make_async_copy(mat.at[:, pl.ds(col, HALF)], buf.at[i, n], sem.at[i, n])
            for i, mat in enumerate((fock, ladder))
        ]

    jobs = [copies(n) for n in range(count)]
    for job in jobs:
        for copy in job:
            copy.start()
    for n, job in enumerate(jobs):
        for i, copy in enumerate(job):
            copy.wait()
            for r in range(SPLIT):
                for q in range(SPLIT):
                    block = buf[i, n, r * TILE : (r + 1) * TILE, q * TILE : (q + 1) * TILE]
                    for p in range(pairs):
                        keep = mask_ref[p * SPLIT + r, slot_ref[n] + q] != 0
                        out_ref[
                            p,
                            i * HALF + r * TILE : i * HALF + (r + 1) * TILE,
                            n * HALF + q * TILE : n * HALF + (q + 1) * TILE,
                        ] = jnp.where(keep, block, jnp.zeros_like(block))


def screened(slot_tiles, masks, fock, ladder, pairs):
    smem = pl.BlockSpec(memory_space=pltpu.SMEM)
    anywhere = pl.BlockSpec(memory_space=pl.ANY)
    count, dtype = slot_tiles.shape[0], fock.dtype
    return pl.pallas_call(
        functools.partial(screen_kernel, pairs),
        out_shape=jax.ShapeDtypeStruct((pairs, 2 * HALF, count * HALF), dtype),
        in_specs=[smem, smem, anywhere, anywhere],
        out_specs=pl.BlockSpec(memory_space=pltpu.VMEM),
        scratch_shapes=[pltpu.VMEM((2, count, HALF, HALF), dtype), pltpu.SemaphoreType.DMA((2, count))],
        compiler_params=pltpu.CompilerParams(vmem_limit_bytes=VMEM_LIMIT),
        cost_estimate=pl.CostEstimate(flops=0, bytes_accessed=4 << 20, transcendentals=0),
        name="screened",
    )(slot_tiles, masks, fock, ladder)


def sum_kernel(pairs, slots, has_acc, finish, *refs):
    refs = list(refs)
    take = lambda n: [refs.pop(0) for _ in range(n)]
    mat, blocks = take(1)[0], take(len(slots))
    acc_in = take(1)[0] if has_acc else None
    couple_ref = take(1)[0] if finish else None
    out, a_buf = refs
    lo, depth = slots[0] * HALF, len(slots) * HALF
    for p in range(pairs):
        for n, block in enumerate(blocks):
            a_buf[n * HALF : (n + 1) * HALF, :] = block[p]
        acc = jnp.dot(mat[p, :, lo : lo + depth], a_buf[...], preferred_element_type=jnp.float32)
        if has_acc:
            acc = acc_in[p] + acc
        if finish:
            lad = acc[HALF:, :].astype(jnp.bfloat16)
            acc = acc[:HALF, :] + jnp.dot(lad, couple_ref[...], preferred_element_type=jnp.float32)
        out[p] = acc.astype(out.dtype)


def sum_slots(name, mat, blocks, first, acc=None, couple=None):
    pairs, _, width = blocks[0].shape
    slots, finish = tuple(range(first, first + len(blocks))), couple is not None
    vmem = pl.BlockSpec(memory_space=pltpu.VMEM)
    operands = [mat, *blocks] + ([acc] if acc is not None else []) + ([couple] if finish else [])
    out_shape = jax.ShapeDtypeStruct((pairs, HALF if finish else 2 * HALF, width), jnp.bfloat16 if finish else jnp.float32)
    flops = 2 * pairs * 2 * HALF * width * (len(slots) * HALF + (width // 2 if finish else 0))
    return pl.pallas_call(
        functools.partial(sum_kernel, pairs, slots, acc is not None, finish),
        out_shape=out_shape,
        in_specs=[vmem] * len(operands),
        out_specs=vmem,
        scratch_shapes=[pltpu.VMEM((len(slots) * HALF, width), blocks[0].dtype)],
        compiler_params=pltpu.CompilerParams(vmem_limit_bytes=VMEM_LIMIT),
        cost_estimate=pl.CostEstimate(flops=flops, bytes_accessed=1 << 20, transcendentals=0),
        name=name,
    )(*operands)


def per_device(amps, fock, ladder, couple, tile_list):
    chips = lax.axis_size("virt") // 2
    total_tiles = fock.shape[1] // TILE
    pairs, _, nnz = tile_list.shape
    place = lax.axis_index("virt")
    chip, core = place // 2, place % 2

    hops = jnp.array([HOPS[abs(n)][0] * (-1 if n < 0 else 1) for n in ORDER], dtype=jnp.int32)
    other = jnp.array([HOPS[abs(n)][1] ^ (n < 0) for n in ORDER], dtype=jnp.int32)
    way = jnp.where(core == 0, -1, 1)
    half_of = jnp.where(other == 1, 1 - core, core)
    slot_tiles = ((chip + way * hops + chips) % chips * 2 * SPLIT + half_of * SPLIT).astype(jnp.int32)
    columns = jnp.arange(total_tiles, dtype=jnp.int32)
    masks = jnp.any(tile_list.reshape(pairs * SPLIT, nnz)[:, :, None] == columns, axis=1).astype(jnp.int32)

    x0 = amps
    x1, s1 = ring_step(x0), ring_step(x0, cross=1)
    mat = screened(slot_tiles, masks, fock, ladder, pairs)
    x2, s2 = ring_step(after(x1, mat)), ring_step(s1)
    acc = sum_slots("sum_1", mat, (x0, x1, s1, core_swap(x0)), 0)
    x3, s3 = ring_step(after(x2, acc)), ring_step(s2)
    acc = sum_slots("sum_2", mat, (core_swap(x1), core_swap(s1), x2, s2), 4, acc)
    x4 = ring_step(after(x3, acc))
    acc = sum_slots("sum_3", mat, (core_swap(x2), core_swap(s2), x3), 8, acc)
    acc = sum_slots("sum_4", mat, (core_swap(x3), core_swap(after(s3, acc)), s3, x4), 11, acc)
    half_term = sum_slots("sum_5", mat, (core_swap(x4),), 15, acc, couple)
    mirrored = mirror_swap(half_term)
    return (half_term.astype(jnp.float32) + mirrored.astype(jnp.float32)).astype(jnp.bfloat16)


def solution(mesh):
    in_specs = (
        P("pair", "virt", None),
        P("virt", None),
        P("virt", None),
        P(),
        P("pair", "virt", None),
    )
    out_specs = P("pair", "virt", None)
    return jax.shard_map(
        per_device, mesh=mesh, in_specs=in_specs, out_specs=out_specs, check_vma=False
    )
```

```python
import functools

import jax
import jax.numpy as jnp
from jax import lax
from jax.experimental import pallas as pl
from jax.experimental.pallas import tpu as pltpu
from jax.sharding import PartitionSpec as P

TILE = 128
HALF = 256
SPLIT = HALF // TILE
VMEM_LIMIT = 24 * 1024 * 1024
RING = 16
ADD_FLOPS = 1 << 34
HOPS = (None, (0, 0), (1, 0), (1, 1), (2, 0), (2, 1), (3, 0), (3, 1), (4, 0))
ORDER = (1, 2, 3, -2, -3, 4, 5, -4, -5, 6, -1, -6, -7, 7, 8, -8)


def core_swap(block):
    count = lax.axis_size("virt")
    return lax.ppermute(block, "virt", [(v, v ^ 1) for v in range(count)])


def ring_step(block, cross=0):
    chips = lax.axis_size("virt") // 2
    route = [(2 * c + cross, 2 * ((c + 1) % chips)) for c in range(chips)]
    route += [(2 * c + 1 - cross, 2 * ((c - 1) % chips) + 1) for c in range(chips)]
    return lax.ppermute(block, "virt", route)


def mirror_of(place, count):
    nbits = count.bit_length() - 1
    return count - 1 - sum(((place >> b) & 1) << (nbits - 1 - b) for b in range(nbits))


def mirror_swap(block):
    count, across = lax.axis_size("pair"), lax.axis_size("virt")
    axes, quarter = ("pair", "virt"), RING // 4
    stops = {}
    for row in range(0, count, RING):
        stops[row + quarter - 1] = row + RING // 2 + 1
        stops[row + RING - quarter] = row + RING // 2 - 2
    at = lambda place, v: place * across + v
    legs = [(place, stop, mirror_of(place, count), v) for place, stop in stops.items() for v in range(0, across, 2)]
    detour = {at(place, v) for place, _, _, v in legs}
    direct = [(at(place, v), at(mirror_of(place, count), v)) for place in range(count) for v in range(across)]
    halfway = lax.ppermute(block, axes, [(at(place, v), at(stop, v)) for place, stop, _, v in legs])
    straight = lax.ppermute(block, axes, [leg for leg in direct if leg[0] not in detour])
    return straight, lax.ppermute(halfway, axes, [(at(stop, v), at(end, v)) for _, stop, end, v in legs])


def add_kernel(a_ref, b_ref, out_ref):
    out_ref[...] = (a_ref[...].astype(jnp.float32) + b_ref[...].astype(jnp.float32)).astype(out_ref.dtype)


def add(a, b):
    vmem = pl.BlockSpec(memory_space=pltpu.VMEM)
    return pl.pallas_call(
        add_kernel,
        out_shape=jax.ShapeDtypeStruct(a.shape, a.dtype),
        in_specs=[vmem, vmem],
        out_specs=vmem,
        cost_estimate=pl.CostEstimate(flops=ADD_FLOPS, bytes_accessed=1 << 20, transcendentals=0),
        name="add",
    )(a, b)


def after(block, *earlier):
    return lax.optimization_barrier((block, *earlier))[0]


def screen_kernel(pairs, slot_ref, mask_ref, fock, ladder, out_ref):
    for n in range(out_ref.shape[2] // HALF):
        for q in range(SPLIT):
            tile = slot_ref[n] + q
            columns = pl.ds(pl.multiple_of(tile * TILE, TILE), TILE)
            for r in range(SPLIT):
                keep = [mask_ref[p * SPLIT + r, tile] != 0 for p in range(pairs)]
                for i, mat in enumerate((fock, ladder)):
                    block = mat[r * TILE : (r + 1) * TILE, columns]
                    for p in range(pairs):
                        out_ref[
                            p,
                            i * HALF + r * TILE : i * HALF + (r + 1) * TILE,
                            n * HALF + q * TILE : n * HALF + (q + 1) * TILE,
                        ] = jnp.where(keep[p], block, jnp.zeros_like(block))


def screened(slot_tiles, masks, fock, ladder, pairs):
    smem = pl.BlockSpec(memory_space=pltpu.SMEM)
    vmem = pl.BlockSpec(memory_space=pltpu.VMEM)
    count, dtype = slot_tiles.shape[0], fock.dtype
    return pl.pallas_call(
        functools.partial(screen_kernel, pairs),
        out_shape=jax.ShapeDtypeStruct((pairs, 2 * HALF, count * HALF), dtype),
        in_specs=[smem, smem, vmem, vmem],
        out_specs=vmem,
        compiler_params=pltpu.CompilerParams(vmem_limit_bytes=VMEM_LIMIT),
        cost_estimate=pl.CostEstimate(flops=0, bytes_accessed=4 << 20, transcendentals=0),
        name="screened",
    )(slot_tiles, masks, fock, ladder)


def sum_kernel(pairs, slots, has_acc, finish, *refs):
    refs = list(refs)
    take = lambda n: [refs.pop(0) for _ in range(n)]
    mat, blocks = take(1)[0], take(len(slots))
    acc_in = take(1)[0] if has_acc else None
    couple_ref = take(1)[0] if finish else None
    out, a_buf = refs
    lo, depth = slots[0] * HALF, len(slots) * HALF
    for p in range(pairs):
        for n, block in enumerate(blocks):
            a_buf[n * HALF : (n + 1) * HALF, :] = block[p]
        acc = jnp.dot(mat[p, :, lo : lo + depth], a_buf[...], preferred_element_type=jnp.float32)
        if has_acc:
            acc = acc_in[p] + acc
        if finish:
            lad = acc[HALF:, :].astype(jnp.bfloat16)
            acc = acc[:HALF, :] + jnp.dot(lad, couple_ref[...], preferred_element_type=jnp.float32)
        out[p] = acc.astype(out.dtype)


def sum_slots(name, mat, blocks, first, acc=None, couple=None):
    pairs, _, width = blocks[0].shape
    slots, finish = tuple(range(first, first + len(blocks))), couple is not None
    vmem = pl.BlockSpec(memory_space=pltpu.VMEM)
    operands = [mat, *blocks] + ([acc] if acc is not None else []) + ([couple] if finish else [])
    out_shape = jax.ShapeDtypeStruct((pairs, HALF if finish else 2 * HALF, width), jnp.bfloat16 if finish else jnp.float32)
    flops = 2 * pairs * 2 * HALF * width * (len(slots) * HALF + (width // 2 if finish else 0))
    return pl.pallas_call(
        functools.partial(sum_kernel, pairs, slots, acc is not None, finish),
        out_shape=out_shape,
        in_specs=[vmem] * len(operands),
        out_specs=vmem,
        scratch_shapes=[pltpu.VMEM((len(slots) * HALF, width), blocks[0].dtype)],
        compiler_params=pltpu.CompilerParams(vmem_limit_bytes=VMEM_LIMIT),
        cost_estimate=pl.CostEstimate(flops=flops, bytes_accessed=1 << 20, transcendentals=0),
        name=name,
    )(*operands)


def per_device(amps, fock, ladder, couple, tile_list):
    chips = lax.axis_size("virt") // 2
    total_tiles = fock.shape[1] // TILE
    pairs, _, nnz = tile_list.shape
    place = lax.axis_index("virt")
    chip, core = place // 2, place % 2

    hops = jnp.array([HOPS[abs(n)][0] * (-1 if n < 0 else 1) for n in ORDER], dtype=jnp.int32)
    other = jnp.array([HOPS[abs(n)][1] ^ (n < 0) for n in ORDER], dtype=jnp.int32)
    way = jnp.where(core == 0, -1, 1)
    half_of = jnp.where(other == 1, 1 - core, core)
    slot_tiles = ((chip + way * hops + chips) % chips * 2 * SPLIT + half_of * SPLIT).astype(jnp.int32)
    columns = jnp.arange(total_tiles, dtype=jnp.int32)
    masks = jnp.any(tile_list.reshape(pairs * SPLIT, nnz)[:, :, None] == columns, axis=1).astype(jnp.int32)

    x0 = amps
    x1, s1 = ring_step(x0), ring_step(x0, cross=1)
    mat = screened(slot_tiles, masks, fock, ladder, pairs)
    x2, s2 = ring_step(after(x1, mat)), ring_step(s1)
    acc = sum_slots("sum_1", mat, (x0, x1, s1), 0)
    x3, s3 = ring_step(after(x2, acc)), ring_step(s2)
    acc = sum_slots("sum_2", mat, (core_swap(x1), core_swap(s1), x2, s2), 3, acc)
    x4 = ring_step(after(x3, acc))
    acc = sum_slots("sum_3", mat, (core_swap(x2), core_swap(s2), x3), 7, acc)
    late = (core_swap(after(x0, acc)), core_swap(x3), core_swap(after(s3, acc)), s3, x4)
    acc = sum_slots("sum_4", mat, late, 10, acc)
    half_term = sum_slots("sum_5", mat, (core_swap(x4),), 15, acc, couple)
    straight, detoured = mirror_swap(half_term)
    return (add(half_term, straight).astype(jnp.float32) + detoured.astype(jnp.float32)).astype(jnp.bfloat16)


def solution(mesh):
    in_specs = (
        P("pair", "virt", None),
        P("virt", None),
        P("virt", None),
        P(),
        P("pair", "virt", None),
    )
    out_specs = P("pair", "virt", None)
    return jax.shard_map(
        per_device, mesh=mesh, in_specs=in_specs, out_specs=out_specs, check_vma=False
    )
```

```python
import functools

import jax
import jax.numpy as jnp
from jax import lax
from jax.experimental import pallas as pl
from jax.experimental.pallas import tpu as pltpu
from jax.sharding import PartitionSpec as P

TILE = 128
HALF = 256
SPLIT = HALF // TILE
VMEM_LIMIT = 24 * 1024 * 1024
RING = 16
HOPS = (None, (0, 0), (1, 0), (1, 1), (2, 0), (2, 1), (3, 0), (3, 1), (4, 0))
ORDER = (1, 2, 3, -2, -3, 4, 5, -4, -5, 6, -1, -6, -7, 7, 8, -8)


def core_swap(block):
    count = lax.axis_size("virt")
    return lax.ppermute(block, "virt", [(v, v ^ 1) for v in range(count)])


def ring_step(block, cross=0):
    chips = lax.axis_size("virt") // 2
    route = [(2 * c + cross, 2 * ((c + 1) % chips)) for c in range(chips)]
    route += [(2 * c + 1 - cross, 2 * ((c - 1) % chips) + 1) for c in range(chips)]
    return lax.ppermute(block, "virt", route)


def mirror_of(place, count):
    nbits = count.bit_length() - 1
    return count - 1 - sum(((place >> b) & 1) << (nbits - 1 - b) for b in range(nbits))


def mirror_swap(block):
    count, across = lax.axis_size("pair"), lax.axis_size("virt")
    axes, quarter = ("pair", "virt"), RING // 4
    stops = {}
    for row in range(0, count, RING):
        stops[row + quarter - 1] = row + RING // 2 + 1
        stops[row + RING - quarter] = row + RING // 2 - 2
    at = lambda place, v: place * across + v
    legs = [(place, stop, mirror_of(place, count), v) for place, stop in stops.items() for v in range(0, across, 2)]
    detour = {at(place, v) for place, _, _, v in legs}
    direct = [(at(place, v), at(mirror_of(place, count), v)) for place in range(count) for v in range(across)]
    halfway = lax.ppermute(block, axes, [(at(place, v), at(stop, v)) for place, stop, _, v in legs])
    straight = lax.ppermute(block, axes, [leg for leg in direct if leg[0] not in detour])
    return straight, lax.ppermute(halfway, axes, [(at(stop, v), at(end, v)) for _, stop, end, v in legs])


def after(block, *earlier):
    return lax.optimization_barrier((block, *earlier))[0]


def screen_kernel(pairs, slot_ref, mask_ref, fock, ladder, out_ref):
    for n in range(out_ref.shape[2] // HALF):
        for q in range(SPLIT):
            tile = slot_ref[n] + q
            columns = pl.ds(pl.multiple_of(tile * TILE, TILE), TILE)
            for r in range(SPLIT):
                keep = [mask_ref[p * SPLIT + r, tile] != 0 for p in range(pairs)]
                for i, mat in enumerate((fock, ladder)):
                    block = mat[r * TILE : (r + 1) * TILE, columns]
                    for p in range(pairs):
                        out_ref[
                            p,
                            i * HALF + r * TILE : i * HALF + (r + 1) * TILE,
                            n * HALF + q * TILE : n * HALF + (q + 1) * TILE,
                        ] = jnp.where(keep[p], block, jnp.zeros_like(block))


def screened(slot_tiles, masks, fock, ladder, pairs):
    smem = pl.BlockSpec(memory_space=pltpu.SMEM)
    vmem = pl.BlockSpec(memory_space=pltpu.VMEM)
    count, dtype = slot_tiles.shape[0], fock.dtype
    return pl.pallas_call(
        functools.partial(screen_kernel, pairs),
        out_shape=jax.ShapeDtypeStruct((pairs, 2 * HALF, count * HALF), dtype),
        in_specs=[smem, smem, vmem, vmem],
        out_specs=vmem,
        compiler_params=pltpu.CompilerParams(vmem_limit_bytes=VMEM_LIMIT),
        cost_estimate=pl.CostEstimate(flops=0, bytes_accessed=4 << 20, transcendentals=0),
        name="screened",
    )(slot_tiles, masks, fock, ladder)


def sum_kernel(pairs, slots, has_acc, finish, *refs):
    refs = list(refs)
    take = lambda n: [refs.pop(0) for _ in range(n)]
    mat, blocks = take(1)[0], take(len(slots))
    acc_in = take(1)[0] if has_acc else None
    couple_ref = take(1)[0] if finish else None
    out, a_buf = refs
    lo, depth = slots[0] * HALF, len(slots) * HALF
    for p in range(pairs):
        for n, block in enumerate(blocks):
            a_buf[n * HALF : (n + 1) * HALF, :] = block[p]
        acc = jnp.dot(mat[p, :, lo : lo + depth], a_buf[...], preferred_element_type=jnp.float32)
        if has_acc:
            acc = acc_in[p] + acc
        if finish:
            lad = acc[HALF:, :].astype(jnp.bfloat16)
            acc = acc[:HALF, :] + jnp.dot(lad, couple_ref[...], preferred_element_type=jnp.float32)
        out[p] = acc.astype(out.dtype)


def sum_slots(name, mat, blocks, first, acc=None, couple=None):
    pairs, _, width = blocks[0].shape
    slots, finish = tuple(range(first, first + len(blocks))), couple is not None
    vmem = pl.BlockSpec(memory_space=pltpu.VMEM)
    operands = [mat, *blocks] + ([acc] if acc is not None else []) + ([couple] if finish else [])
    out_shape = jax.ShapeDtypeStruct((pairs, HALF if finish else 2 * HALF, width), jnp.bfloat16 if finish else jnp.float32)
    flops = 2 * pairs * 2 * HALF * width * (len(slots) * HALF + (width // 2 if finish else 0))
    return pl.pallas_call(
        functools.partial(sum_kernel, pairs, slots, acc is not None, finish),
        out_shape=out_shape,
        in_specs=[vmem] * len(operands),
        out_specs=vmem,
        scratch_shapes=[pltpu.VMEM((len(slots) * HALF, width), blocks[0].dtype)],
        compiler_params=pltpu.CompilerParams(vmem_limit_bytes=VMEM_LIMIT),
        cost_estimate=pl.CostEstimate(flops=flops, bytes_accessed=1 << 20, transcendentals=0),
        name=name,
    )(*operands)


def per_device(amps, fock, ladder, couple, tile_list):
    chips = lax.axis_size("virt") // 2
    total_tiles = fock.shape[1] // TILE
    pairs, _, nnz = tile_list.shape
    place = lax.axis_index("virt")
    chip, core = place // 2, place % 2

    hops = jnp.array([HOPS[abs(n)][0] * (-1 if n < 0 else 1) for n in ORDER], dtype=jnp.int32)
    other = jnp.array([HOPS[abs(n)][1] ^ (n < 0) for n in ORDER], dtype=jnp.int32)
    way = jnp.where(core == 0, -1, 1)
    half_of = jnp.where(other == 1, 1 - core, core)
    slot_tiles = ((chip + way * hops + chips) % chips * 2 * SPLIT + half_of * SPLIT).astype(jnp.int32)
    columns = jnp.arange(total_tiles, dtype=jnp.int32)
    masks = jnp.any(tile_list.reshape(pairs * SPLIT, nnz)[:, :, None] == columns, axis=1).astype(jnp.int32)

    x0 = amps
    x1, s1 = ring_step(x0), ring_step(x0, cross=1)
    mat = screened(slot_tiles, masks, fock, ladder, pairs)
    x2, s2 = ring_step(after(x1, mat)), ring_step(s1)
    acc = sum_slots("sum_1", mat, (x0, x1, s1), 0)
    x3, s3 = ring_step(after(x2, acc)), ring_step(s2)
    acc = sum_slots("sum_2", mat, (core_swap(x1), core_swap(s1), x2, s2), 3, acc)
    x4 = ring_step(after(x3, acc))
    acc = sum_slots("sum_3", mat, (core_swap(x2), core_swap(s2), x3), 7, acc)
    late = (core_swap(after(x0, acc)), core_swap(x3), core_swap(after(s3, acc)), s3, x4)
    acc = sum_slots("sum_4", mat, late, 10, acc)
    half_term = sum_slots("sum_5", mat, (core_swap(x4),), 15, acc, couple)
    terms = [term.astype(jnp.float32) for term in (half_term, *mirror_swap(half_term))]
    return (terms[0] + (terms[1] + terms[2])).astype(jnp.bfloat16)


def solution(mesh):
    in_specs = (
        P("pair", "virt", None),
        P("virt", None),
        P("virt", None),
        P(),
        P("pair", "virt", None),
    )
    out_specs = P("pair", "virt", None)
    return jax.shard_map(
        per_device, mesh=mesh, in_specs=in_specs, out_specs=out_specs, check_vma=False
    )
```

```python
import functools

import jax
import jax.numpy as jnp
from jax import lax
from jax.experimental import pallas as pl
from jax.experimental.pallas import tpu as pltpu
from jax.sharding import PartitionSpec as P

TILE = 128
HALF = 256
SPLIT = HALF // TILE
VMEM_LIMIT = 24 * 1024 * 1024
RING = 16
HOPS = (None, (0, 0), (1, 0), (1, 1), (2, 0), (2, 1), (3, 0), (3, 1), (4, 0))
ORDER = (1, 2, 3, -2, -3, 4, 5, -4, -5, 6, -1, -6, -7, 7, 8, -8)


def core_swap(block):
    count = lax.axis_size("virt")
    return lax.ppermute(block, "virt", [(v, v ^ 1) for v in range(count)])


def ring_step(block, cross=0):
    chips = lax.axis_size("virt") // 2
    route = [(2 * c + cross, 2 * ((c + 1) % chips)) for c in range(chips)]
    route += [(2 * c + 1 - cross, 2 * ((c - 1) % chips) + 1) for c in range(chips)]
    return lax.ppermute(block, "virt", route)


def mirror_of(place, count):
    nbits = count.bit_length() - 1
    return count - 1 - sum(((place >> b) & 1) << (nbits - 1 - b) for b in range(nbits))


def detours(rows):
    moves = []
    for x in range(rows):
        for core in range(2):
            moves.append(((x, RING // 4 - 1), (x, RING // 2), core))
            moves.append(((x, RING - RING // 4), (x, RING // 2 - 1), core))
    for z, row in ((5, 1), (6, 2), (9, 1), (10, 2)):
        moves.append(((0, z), (row, z), 0))
        moves.append(((rows - 1, RING - 1 - z), (rows - 1 - row, RING - 1 - z), 1))
    return [(place[0] * RING + place[1], stop[0] * RING + stop[1], core) for place, stop, core in moves]


def mirror_swap(block):
    count, across = lax.axis_size("pair"), lax.axis_size("virt")
    axes = ("pair", "virt")
    first, second, direct = [], [], []
    moves = {(place, core): stop for place, stop, core in detours(count // RING)}
    for place in range(count):
        for v in range(across):
            here, end = place * across + v, mirror_of(place, count) * across + v
            if (place, v % 2) in moves:
                stop = moves[place, v % 2] * across + v
                first.append((here, stop))
                second.append((stop, end))
            else:
                direct.append((here, end))
    halfway = lax.ppermute(block, axes, first)
    straight = lax.ppermute(block, axes, direct)
    return straight, lax.ppermute(halfway, axes, second)


def after(block, *earlier):
    return lax.optimization_barrier((block, *earlier))[0]


def screen_kernel(pairs, slot_ref, mask_ref, fock, ladder, out_ref):
    for n in range(out_ref.shape[2] // HALF):
        for q in range(SPLIT):
            tile = slot_ref[n] + q
            columns = pl.ds(pl.multiple_of(tile * TILE, TILE), TILE)
            for r in range(SPLIT):
                keep = [mask_ref[p * SPLIT + r, tile] != 0 for p in range(pairs)]
                for i, mat in enumerate((fock, ladder)):
                    block = mat[r * TILE : (r + 1) * TILE, columns]
                    for p in range(pairs):
                        out_ref[
                            p,
                            i * HALF + r * TILE : i * HALF + (r + 1) * TILE,
                            n * HALF + q * TILE : n * HALF + (q + 1) * TILE,
                        ] = jnp.where(keep[p], block, jnp.zeros_like(block))


def screened(slot_tiles, masks, fock, ladder, pairs):
    smem = pl.BlockSpec(memory_space=pltpu.SMEM)
    vmem = pl.BlockSpec(memory_space=pltpu.VMEM)
    count, dtype = slot_tiles.shape[0], fock.dtype
    return pl.pallas_call(
        functools.partial(screen_kernel, pairs),
        out_shape=jax.ShapeDtypeStruct((pairs, 2 * HALF, count * HALF), dtype),
        in_specs=[smem, smem, vmem, vmem],
        out_specs=vmem,
        compiler_params=pltpu.CompilerParams(vmem_limit_bytes=VMEM_LIMIT),
        cost_estimate=pl.CostEstimate(flops=0, bytes_accessed=4 << 20, transcendentals=0),
        name="screened",
    )(slot_tiles, masks, fock, ladder)


def sum_kernel(pairs, slots, has_acc, finish, *refs):
    refs = list(refs)
    take = lambda n: [refs.pop(0) for _ in range(n)]
    mat, blocks = take(1)[0], take(len(slots))
    acc_in = take(1)[0] if has_acc else None
    couple_ref = take(1)[0] if finish else None
    out, a_buf = refs
    lo, depth = slots[0] * HALF, len(slots) * HALF
    for p in range(pairs):
        for n, block in enumerate(blocks):
            a_buf[n * HALF : (n + 1) * HALF, :] = block[p]
        acc = jnp.dot(mat[p, :, lo : lo + depth], a_buf[...], preferred_element_type=jnp.float32)
        if has_acc:
            acc = acc_in[p] + acc
        if finish:
            lad = acc[HALF:, :].astype(jnp.bfloat16)
            acc = acc[:HALF, :] + jnp.dot(lad, couple_ref[...], preferred_element_type=jnp.float32)
        out[p] = acc.astype(out.dtype)


def sum_slots(name, mat, blocks, first, acc=None, couple=None):
    pairs, _, width = blocks[0].shape
    slots, finish = tuple(range(first, first + len(blocks))), couple is not None
    vmem = pl.BlockSpec(memory_space=pltpu.VMEM)
    operands = [mat, *blocks] + ([acc] if acc is not None else []) + ([couple] if finish else [])
    out_shape = jax.ShapeDtypeStruct((pairs, HALF if finish else 2 * HALF, width), jnp.bfloat16 if finish else jnp.float32)
    flops = 2 * pairs * 2 * HALF * width * (len(slots) * HALF + (width // 2 if finish else 0))
    return pl.pallas_call(
        functools.partial(sum_kernel, pairs, slots, acc is not None, finish),
        out_shape=out_shape,
        in_specs=[vmem] * len(operands),
        out_specs=vmem,
        scratch_shapes=[pltpu.VMEM((len(slots) * HALF, width), blocks[0].dtype)],
        compiler_params=pltpu.CompilerParams(vmem_limit_bytes=VMEM_LIMIT),
        cost_estimate=pl.CostEstimate(flops=flops, bytes_accessed=1 << 20, transcendentals=0),
        name=name,
    )(*operands)


def per_device(amps, fock, ladder, couple, tile_list):
    chips = lax.axis_size("virt") // 2
    total_tiles = fock.shape[1] // TILE
    pairs, _, nnz = tile_list.shape
    place = lax.axis_index("virt")
    chip, core = place // 2, place % 2

    hops = jnp.array([HOPS[abs(n)][0] * (-1 if n < 0 else 1) for n in ORDER], dtype=jnp.int32)
    other = jnp.array([HOPS[abs(n)][1] ^ (n < 0) for n in ORDER], dtype=jnp.int32)
    way = jnp.where(core == 0, -1, 1)
    half_of = jnp.where(other == 1, 1 - core, core)
    slot_tiles = ((chip + way * hops + chips) % chips * 2 * SPLIT + half_of * SPLIT).astype(jnp.int32)
    columns = jnp.arange(total_tiles, dtype=jnp.int32)
    masks = jnp.any(tile_list.reshape(pairs * SPLIT, nnz)[:, :, None] == columns, axis=1).astype(jnp.int32)

    x0 = amps
    x1, s1 = ring_step(x0), ring_step(x0, cross=1)
    mat = screened(slot_tiles, masks, fock, ladder, pairs)
    x2, s2 = ring_step(after(x1, mat)), ring_step(s1)
    acc = sum_slots("sum_1", mat, (x0, x1, s1), 0)
    x3, s3 = ring_step(after(x2, acc)), ring_step(s2)
    acc = sum_slots("sum_2", mat, (core_swap(x1), core_swap(s1), x2, s2), 3, acc)
    x4 = ring_step(after(x3, acc))
    acc = sum_slots("sum_3", mat, (core_swap(x2), core_swap(s2), x3, core_swap(x0)), 7, acc)
    acc = sum_slots("sum_4", mat, (core_swap(x3), core_swap(s3), s3, x4), 11, acc)
    half_term = sum_slots("sum_5", mat, (core_swap(x4),), 15, acc, couple)
    terms = [term.astype(jnp.float32) for term in (half_term, *mirror_swap(half_term))]
    return (terms[0] + (terms[1] + terms[2])).astype(jnp.bfloat16)


def solution(mesh):
    in_specs = (
        P("pair", "virt", None),
        P("virt", None),
        P("virt", None),
        P(),
        P("pair", "virt", None),
    )
    out_specs = P("pair", "virt", None)
    return jax.shard_map(
        per_device, mesh=mesh, in_specs=in_specs, out_specs=out_specs, check_vma=False
    )
```

```python
import functools

import jax
import jax.numpy as jnp
from jax import lax
from jax.experimental import pallas as pl
from jax.experimental.pallas import tpu as pltpu
from jax.sharding import PartitionSpec as P

TILE = 128
HALF = 256
SPLIT = HALF // TILE
VMEM_LIMIT = 24 * 1024 * 1024
RING = 16
MARK_FLOPS = 1 << 33
HOPS = (None, (0, 0), (1, 0), (1, 1), (2, 0), (2, 1), (3, 0), (3, 1), (4, 0))
ORDER = (1, 2, 3, -2, -3, 4, 5, -4, -5, 6, -1, -6, -7, 7, 8, -8)


def core_swap(block):
    count = lax.axis_size("virt")
    return lax.ppermute(block, "virt", [(v, v ^ 1) for v in range(count)])


def ring_step(block, cross=0):
    chips = lax.axis_size("virt") // 2
    route = [(2 * c + cross, 2 * ((c + 1) % chips)) for c in range(chips)]
    route += [(2 * c + 1 - cross, 2 * ((c - 1) % chips) + 1) for c in range(chips)]
    return lax.ppermute(block, "virt", route)


def mirror_of(place, count):
    nbits = count.bit_length() - 1
    return count - 1 - sum(((place >> b) & 1) << (nbits - 1 - b) for b in range(nbits))


def detours(rows):
    moves = []
    for x in range(rows):
        for core in range(2):
            moves.append(((x, RING // 4 - 1), (x, RING // 2), core))
            moves.append(((x, RING - RING // 4), (x, RING // 2 - 1), core))
    for z, row in ((5, 1), (6, 2), (9, 1), (10, 2)):
        moves.append(((0, z), (row, z), 0))
        moves.append(((rows - 1, RING - 1 - z), (rows - 1 - row, RING - 1 - z), 1))
    return [(place[0] * RING + place[1], stop[0] * RING + stop[1], core) for place, stop, core in moves]


def mirror_swap(block):
    count, across = lax.axis_size("pair"), lax.axis_size("virt")
    axes = ("pair", "virt")
    first, second, direct = [], [], []
    moves = {(place, core): stop for place, stop, core in detours(count // RING)}
    for place in range(count):
        for v in range(across):
            here, end = place * across + v, mirror_of(place, count) * across + v
            if (place, v % 2) in moves:
                stop = moves[place, v % 2] * across + v
                first.append((here, stop))
                second.append((stop, end))
            else:
                direct.append((here, end))
    halfway = lax.ppermute(block, axes, first)
    straight = lax.ppermute(block, axes, direct)
    return straight, lax.ppermute(halfway, axes, second)


def after(block, *earlier):
    return lax.optimization_barrier((block, *earlier))[0]


def mark_kernel(list_ref, out_ref):
    listed = list_ref[...]
    columns = lax.broadcasted_iota(jnp.int32, out_ref.shape, 1)
    hit = columns == listed[:, 0:1]
    for n in range(1, listed.shape[1]):
        hit = hit | (columns == listed[:, n : n + 1])
    out_ref[...] = hit.astype(jnp.int32)


def marks(listed, total_tiles):
    vmem = pl.BlockSpec(memory_space=pltpu.VMEM)
    return pl.pallas_call(
        mark_kernel,
        out_shape=jax.ShapeDtypeStruct((listed.shape[0], total_tiles), jnp.int32),
        in_specs=[vmem],
        out_specs=vmem,
        cost_estimate=pl.CostEstimate(flops=MARK_FLOPS, bytes_accessed=1 << 12, transcendentals=0),
        name="marks",
    )(listed)


def screen_kernel(pairs, slot_ref, mask_ref, fock, ladder, out_ref):
    for n in range(out_ref.shape[2] // HALF):
        for q in range(SPLIT):
            tile = slot_ref[n] + q
            columns = pl.ds(pl.multiple_of(tile * TILE, TILE), TILE)
            for r in range(SPLIT):
                keep = [mask_ref[p * SPLIT + r, tile] != 0 for p in range(pairs)]
                for i, mat in enumerate((fock, ladder)):
                    block = mat[r * TILE : (r + 1) * TILE, columns]
                    for p in range(pairs):
                        out_ref[
                            p,
                            i * HALF + r * TILE : i * HALF + (r + 1) * TILE,
                            n * HALF + q * TILE : n * HALF + (q + 1) * TILE,
                        ] = jnp.where(keep[p], block, jnp.zeros_like(block))


def screened(slot_tiles, masks, fock, ladder, pairs):
    smem = pl.BlockSpec(memory_space=pltpu.SMEM)
    vmem = pl.BlockSpec(memory_space=pltpu.VMEM)
    count, dtype = slot_tiles.shape[0], fock.dtype
    return pl.pallas_call(
        functools.partial(screen_kernel, pairs),
        out_shape=jax.ShapeDtypeStruct((pairs, 2 * HALF, count * HALF), dtype),
        in_specs=[smem, smem, vmem, vmem],
        out_specs=vmem,
        compiler_params=pltpu.CompilerParams(vmem_limit_bytes=VMEM_LIMIT),
        cost_estimate=pl.CostEstimate(flops=0, bytes_accessed=4 << 20, transcendentals=0),
        name="screened",
    )(slot_tiles, masks, fock, ladder)


def sum_kernel(pairs, slots, has_acc, finish, *refs):
    refs = list(refs)
    take = lambda n: [refs.pop(0) for _ in range(n)]
    mat, blocks = take(1)[0], take(len(slots))
    acc_in = take(1)[0] if has_acc else None
    couple_ref = take(1)[0] if finish else None
    out, a_buf = refs
    lo, depth = slots[0] * HALF, len(slots) * HALF
    for p in range(pairs):
        for n, block in enumerate(blocks):
            a_buf[n * HALF : (n + 1) * HALF, :] = block[p]
        acc = jnp.dot(mat[p, :, lo : lo + depth], a_buf[...], preferred_element_type=jnp.float32)
        if has_acc:
            acc = acc_in[p] + acc
        if finish:
            lad = acc[HALF:, :].astype(jnp.bfloat16)
            acc = acc[:HALF, :] + jnp.dot(lad, couple_ref[...], preferred_element_type=jnp.float32)
        out[p] = acc.astype(out.dtype)


def sum_slots(name, mat, blocks, first, acc=None, couple=None):
    pairs, _, width = blocks[0].shape
    slots, finish = tuple(range(first, first + len(blocks))), couple is not None
    vmem = pl.BlockSpec(memory_space=pltpu.VMEM)
    operands = [mat, *blocks] + ([acc] if acc is not None else []) + ([couple] if finish else [])
    out_shape = jax.ShapeDtypeStruct((pairs, HALF if finish else 2 * HALF, width), jnp.bfloat16 if finish else jnp.float32)
    flops = 2 * pairs * 2 * HALF * width * (len(slots) * HALF + (width // 2 if finish else 0))
    return pl.pallas_call(
        functools.partial(sum_kernel, pairs, slots, acc is not None, finish),
        out_shape=out_shape,
        in_specs=[vmem] * len(operands),
        out_specs=vmem,
        scratch_shapes=[pltpu.VMEM((len(slots) * HALF, width), blocks[0].dtype)],
        compiler_params=pltpu.CompilerParams(vmem_limit_bytes=VMEM_LIMIT),
        cost_estimate=pl.CostEstimate(flops=flops, bytes_accessed=1 << 20, transcendentals=0),
        name=name,
    )(*operands)


def per_device(amps, fock, ladder, couple, tile_list):
    chips = lax.axis_size("virt") // 2
    total_tiles = fock.shape[1] // TILE
    pairs, _, nnz = tile_list.shape
    place = lax.axis_index("virt")
    chip, core = place // 2, place % 2

    hops = jnp.array([HOPS[abs(n)][0] * (-1 if n < 0 else 1) for n in ORDER], dtype=jnp.int32)
    other = jnp.array([HOPS[abs(n)][1] ^ (n < 0) for n in ORDER], dtype=jnp.int32)
    way = jnp.where(core == 0, -1, 1)
    half_of = jnp.where(other == 1, 1 - core, core)
    slot_tiles = ((chip + way * hops + chips) % chips * 2 * SPLIT + half_of * SPLIT).astype(jnp.int32)
    masks = marks(tile_list.reshape(pairs * SPLIT, nnz), total_tiles)

    x0 = amps
    x1, s1 = ring_step(x0), ring_step(x0, cross=1)
    mat = screened(slot_tiles, masks, fock, ladder, pairs)
    x2, s2 = ring_step(after(x1, mat)), ring_step(s1)
    acc = sum_slots("sum_1", mat, (x0, x1, s1), 0)
    x3, s3 = ring_step(after(x2, acc)), ring_step(s2)
    acc = sum_slots("sum_2", mat, (core_swap(x1), core_swap(s1), x2, s2), 3, acc)
    x4 = ring_step(after(x3, acc))
    acc = sum_slots("sum_3", mat, (core_swap(x2), core_swap(s2), x3, core_swap(x0)), 7, acc)
    acc = sum_slots("sum_4", mat, (core_swap(x3), core_swap(s3), s3, x4), 11, acc)
    half_term = sum_slots("sum_5", mat, (core_swap(x4),), 15, acc, couple)
    terms = [term.astype(jnp.float32) for term in (half_term, *mirror_swap(half_term))]
    return (terms[0] + (terms[1] + terms[2])).astype(jnp.bfloat16)


def solution(mesh):
    in_specs = (
        P("pair", "virt", None),
        P("virt", None),
        P("virt", None),
        P(),
        P("pair", "virt", None),
    )
    out_specs = P("pair", "virt", None)
    return jax.shard_map(
        per_device, mesh=mesh, in_specs=in_specs, out_specs=out_specs, check_vma=False
    )
```

```python
import functools

import jax
import jax.numpy as jnp
from jax import lax
from jax.experimental import pallas as pl
from jax.experimental.pallas import tpu as pltpu
from jax.sharding import PartitionSpec as P

TILE = 128
HALF = 256
SPLIT = HALF // TILE
VMEM_LIMIT = 24 * 1024 * 1024
RING = 16
HOPS = (None, (0, 0), (1, 0), (1, 1), (2, 0), (2, 1), (3, 0), (3, 1), (4, 0))
ORDER = (1, 2, 3, -2, -3, 4, 5, -4, -5, 6, -1, -6, -7, 7, 8, -8)


def core_swap(block):
    count = lax.axis_size("virt")
    return lax.ppermute(block, "virt", [(v, v ^ 1) for v in range(count)])


def ring_step(block, cross=0):
    chips = lax.axis_size("virt") // 2
    route = [(2 * c + cross, 2 * ((c + 1) % chips)) for c in range(chips)]
    route += [(2 * c + 1 - cross, 2 * ((c - 1) % chips) + 1) for c in range(chips)]
    return lax.ppermute(block, "virt", route)


def mirror_of(place, count):
    nbits = count.bit_length() - 1
    return count - 1 - sum(((place >> b) & 1) << (nbits - 1 - b) for b in range(nbits))


def detours(rows):
    moves = []
    for x, z in enumerate((3, 1, 2, 3)):
        for core in range(2):
            moves.append(((x, z), (x, RING // 2), core))
            moves.append(((rows - 1 - x, RING - 1 - z), (rows - 1 - x, RING // 2 - 1), core))
    for z, row in ((5, 1), (6, 2), (9, 1), (10, 2)):
        moves.append(((0, z), (row, z), 0))
        moves.append(((rows - 1, RING - 1 - z), (rows - 1 - row, RING - 1 - z), 1))
    return [(place[0] * RING + place[1], stop[0] * RING + stop[1], core) for place, stop, core in moves]


def mirror_swap(block):
    count, across = lax.axis_size("pair"), lax.axis_size("virt")
    axes = ("pair", "virt")
    first, second, direct = [], [], []
    moves = {(place, core): stop for place, stop, core in detours(count // RING)}
    for place in range(count):
        for v in range(across):
            here, end = place * across + v, mirror_of(place, count) * across + v
            if (place, v % 2) in moves:
                stop = moves[place, v % 2] * across + v
                first.append((here, stop))
                second.append((stop, end))
            else:
                direct.append((here, end))
    halfway = lax.ppermute(block, axes, first)
    straight = lax.ppermute(block, axes, direct)
    return straight, lax.ppermute(halfway, axes, second)


def after(block, *earlier):
    return lax.optimization_barrier((block, *earlier))[0]


def screen_kernel(pairs, slot_ref, mask_ref, fock, ladder, out_ref):
    for n in range(out_ref.shape[2] // HALF):
        for q in range(SPLIT):
            tile = slot_ref[n] + q
            columns = pl.ds(pl.multiple_of(tile * TILE, TILE), TILE)
            for r in range(SPLIT):
                keep = [mask_ref[p * SPLIT + r, tile] != 0 for p in range(pairs)]
                for i, mat in enumerate((fock, ladder)):
                    block = mat[r * TILE : (r + 1) * TILE, columns]
                    for p in range(pairs):
                        out_ref[
                            p,
                            i * HALF + r * TILE : i * HALF + (r + 1) * TILE,
                            n * HALF + q * TILE : n * HALF + (q + 1) * TILE,
                        ] = jnp.where(keep[p], block, jnp.zeros_like(block))


def screened(slot_tiles, masks, fock, ladder, pairs):
    smem = pl.BlockSpec(memory_space=pltpu.SMEM)
    vmem = pl.BlockSpec(memory_space=pltpu.VMEM)
    count, dtype = slot_tiles.shape[0], fock.dtype
    return pl.pallas_call(
        functools.partial(screen_kernel, pairs),
        out_shape=jax.ShapeDtypeStruct((pairs, 2 * HALF, count * HALF), dtype),
        in_specs=[smem, smem, vmem, vmem],
        out_specs=vmem,
        compiler_params=pltpu.CompilerParams(vmem_limit_bytes=VMEM_LIMIT),
        cost_estimate=pl.CostEstimate(flops=0, bytes_accessed=4 << 20, transcendentals=0),
        name="screened",
    )(slot_tiles, masks, fock, ladder)


def sum_kernel(pairs, slots, has_acc, finish, *refs):
    refs = list(refs)
    take = lambda n: [refs.pop(0) for _ in range(n)]
    mat, blocks = take(1)[0], take(len(slots))
    acc_in = take(1)[0] if has_acc else None
    couple_ref = take(1)[0] if finish else None
    out, a_buf = refs
    lo, depth = slots[0] * HALF, len(slots) * HALF
    for p in range(pairs):
        for n, block in enumerate(blocks):
            a_buf[n * HALF : (n + 1) * HALF, :] = block[p]
        acc = jnp.dot(mat[p, :, lo : lo + depth], a_buf[...], preferred_element_type=jnp.float32)
        if has_acc:
            acc = acc_in[p] + acc
        if finish:
            lad = acc[HALF:, :].astype(jnp.bfloat16)
            acc = acc[:HALF, :] + jnp.dot(lad, couple_ref[...], preferred_element_type=jnp.float32)
        out[p] = acc.astype(out.dtype)


def sum_slots(name, mat, blocks, first, acc=None, couple=None):
    pairs, _, width = blocks[0].shape
    slots, finish = tuple(range(first, first + len(blocks))), couple is not None
    vmem = pl.BlockSpec(memory_space=pltpu.VMEM)
    operands = [mat, *blocks] + ([acc] if acc is not None else []) + ([couple] if finish else [])
    out_shape = jax.ShapeDtypeStruct((pairs, HALF if finish else 2 * HALF, width), jnp.bfloat16 if finish else jnp.float32)
    flops = 2 * pairs * 2 * HALF * width * (len(slots) * HALF + (width // 2 if finish else 0))
    return pl.pallas_call(
        functools.partial(sum_kernel, pairs, slots, acc is not None, finish),
        out_shape=out_shape,
        in_specs=[vmem] * len(operands),
        out_specs=vmem,
        scratch_shapes=[pltpu.VMEM((len(slots) * HALF, width), blocks[0].dtype)],
        compiler_params=pltpu.CompilerParams(vmem_limit_bytes=VMEM_LIMIT),
        cost_estimate=pl.CostEstimate(flops=flops, bytes_accessed=1 << 20, transcendentals=0),
        name=name,
    )(*operands)


def per_device(amps, fock, ladder, couple, tile_list):
    chips = lax.axis_size("virt") // 2
    total_tiles = fock.shape[1] // TILE
    pairs, _, nnz = tile_list.shape
    place = lax.axis_index("virt")
    chip, core = place // 2, place % 2

    hops = jnp.array([HOPS[abs(n)][0] * (-1 if n < 0 else 1) for n in ORDER], dtype=jnp.int32)
    other = jnp.array([HOPS[abs(n)][1] ^ (n < 0) for n in ORDER], dtype=jnp.int32)
    way = jnp.where(core == 0, -1, 1)
    half_of = jnp.where(other == 1, 1 - core, core)
    slot_tiles = ((chip + way * hops + chips) % chips * 2 * SPLIT + half_of * SPLIT).astype(jnp.int32)
    columns = jnp.arange(total_tiles, dtype=jnp.int32)
    masks = jnp.any(tile_list.reshape(pairs * SPLIT, nnz)[:, :, None] == columns, axis=1).astype(jnp.int32)

    x0 = amps
    x1, s1 = ring_step(x0), ring_step(x0, cross=1)
    mat = screened(slot_tiles, masks, fock, ladder, pairs)
    x2, s2 = ring_step(after(x1, mat)), ring_step(s1)
    acc = sum_slots("sum_1", mat, (x0, x1, s1), 0)
    x3, s3 = ring_step(after(x2, acc)), ring_step(s2)
    acc = sum_slots("sum_2", mat, (core_swap(x1), core_swap(s1), x2, s2), 3, acc)
    x4 = ring_step(after(x3, acc))
    acc = sum_slots("sum_3", mat, (core_swap(x2), core_swap(s2), x3, core_swap(x0)), 7, acc)
    acc = sum_slots("sum_4", mat, (core_swap(x3), core_swap(s3), s3, x4), 11, acc)
    half_term = sum_slots("sum_5", mat, (core_swap(x4),), 15, acc, couple)
    terms = [term.astype(jnp.float32) for term in (half_term, *mirror_swap(half_term))]
    return (terms[0] + (terms[1] + terms[2])).astype(jnp.bfloat16)


def solution(mesh):
    in_specs = (
        P("pair", "virt", None),
        P("virt", None),
        P("virt", None),
        P(),
        P("pair", "virt", None),
    )
    out_specs = P("pair", "virt", None)
    return jax.shard_map(
        per_device, mesh=mesh, in_specs=in_specs, out_specs=out_specs, check_vma=False
    )
```

```python
import functools

import jax
import jax.numpy as jnp
from jax import lax
from jax.experimental import pallas as pl
from jax.experimental.pallas import tpu as pltpu
from jax.sharding import PartitionSpec as P

TILE = 128
HALF = 256
SPLIT = HALF // TILE
VMEM_LIMIT = 24 * 1024 * 1024
RING = 16
HOPS = (None, (0, 0), (1, 0), (1, 1), (2, 0), (2, 1), (3, 0), (3, 1), (4, 0))
ORDER = (1, 2, 3, -2, -3, 4, 5, -4, -1, -5, 6, -6, -7, 7, 8, -8)


def core_swap(block):
    count = lax.axis_size("virt")
    return lax.ppermute(block, "virt", [(v, v ^ 1) for v in range(count)])


def ring_step(block, cross=0):
    chips = lax.axis_size("virt") // 2
    route = [(2 * c + cross, 2 * ((c + 1) % chips)) for c in range(chips)]
    route += [(2 * c + 1 - cross, 2 * ((c - 1) % chips) + 1) for c in range(chips)]
    return lax.ppermute(block, "virt", route)


def mirror_of(place, count):
    nbits = count.bit_length() - 1
    return count - 1 - sum(((place >> b) & 1) << (nbits - 1 - b) for b in range(nbits))


def detours(rows):
    moves = []
    for x, z in enumerate((3, 1, 2, 3)):
        for core in range(2):
            moves.append(((x, z), (x, RING // 2), core))
            moves.append(((rows - 1 - x, RING - 1 - z), (rows - 1 - x, RING // 2 - 1), core))
    for z, row in ((5, 1), (6, 2), (9, 1), (10, 2)):
        moves.append(((0, z), (row, z), 0))
        moves.append(((rows - 1, RING - 1 - z), (rows - 1 - row, RING - 1 - z), 1))
    return [(place[0] * RING + place[1], stop[0] * RING + stop[1], core) for place, stop, core in moves]


def mirror_swap(block):
    count, across = lax.axis_size("pair"), lax.axis_size("virt")
    axes = ("pair", "virt")
    first, second, direct = [], [], []
    moves = {(place, core): stop for place, stop, core in detours(count // RING)}
    for place in range(count):
        for v in range(across):
            here, end = place * across + v, mirror_of(place, count) * across + v
            if (place, v % 2) in moves:
                stop = moves[place, v % 2] * across + v
                first.append((here, stop))
                second.append((stop, end))
            else:
                direct.append((here, end))
    halfway = lax.ppermute(block, axes, first)
    straight = lax.ppermute(block, axes, direct)
    return straight, lax.ppermute(halfway, axes, second)


def after(block, *earlier):
    return lax.optimization_barrier((block, *earlier))[0]


def screen_kernel(pairs, slot_ref, mask_ref, fock, ladder, out_ref):
    for n in range(out_ref.shape[2] // HALF):
        for q in range(SPLIT):
            tile = slot_ref[n] + q
            columns = pl.ds(pl.multiple_of(tile * TILE, TILE), TILE)
            for r in range(SPLIT):
                keep = [mask_ref[p * SPLIT + r, tile] != 0 for p in range(pairs)]
                for i, mat in enumerate((fock, ladder)):
                    block = mat[r * TILE : (r + 1) * TILE, columns]
                    for p in range(pairs):
                        out_ref[
                            p,
                            i * HALF + r * TILE : i * HALF + (r + 1) * TILE,
                            n * HALF + q * TILE : n * HALF + (q + 1) * TILE,
                        ] = jnp.where(keep[p], block, jnp.zeros_like(block))


def screened(slot_tiles, masks, fock, ladder, pairs):
    smem = pl.BlockSpec(memory_space=pltpu.SMEM)
    vmem = pl.BlockSpec(memory_space=pltpu.VMEM)
    count, dtype = slot_tiles.shape[0], fock.dtype
    return pl.pallas_call(
        functools.partial(screen_kernel, pairs),
        out_shape=jax.ShapeDtypeStruct((pairs, 2 * HALF, count * HALF), dtype),
        in_specs=[smem, smem, vmem, vmem],
        out_specs=vmem,
        compiler_params=pltpu.CompilerParams(vmem_limit_bytes=VMEM_LIMIT),
        cost_estimate=pl.CostEstimate(flops=0, bytes_accessed=4 << 20, transcendentals=0),
        name="screened",
    )(slot_tiles, masks, fock, ladder)


def sum_kernel(pairs, slots, block_count, has_acc, finish, *refs):
    refs = list(refs)
    take = lambda n: [refs.pop(0) for _ in range(n)]
    mat, blocks = take(1)[0], take(block_count)
    acc_in = take(1)[0] if has_acc else None
    couple_ref = take(1)[0] if finish else None
    out, a_buf = refs
    lo, depth = slots[0] * HALF, len(slots) * HALF
    for p in range(pairs):
        held = [block.at[k + p] for block in blocks for k in range(0, block.shape[0], pairs)]
        for n, block in enumerate(held):
            a_buf[n * HALF : (n + 1) * HALF, :] = block[...]
        acc = jnp.dot(mat[p, :, lo : lo + depth], a_buf[...], preferred_element_type=jnp.float32)
        if has_acc:
            acc = acc_in[p] + acc
        if finish:
            lad = acc[HALF:, :].astype(jnp.bfloat16)
            acc = acc[:HALF, :] + jnp.dot(lad, couple_ref[...], preferred_element_type=jnp.float32)
        out[p] = acc.astype(out.dtype)


def sum_slots(name, mat, blocks, first, acc=None, couple=None):
    pairs, width = mat.shape[0], blocks[0].shape[2]
    held = sum(block.shape[0] for block in blocks) // pairs
    slots, finish = tuple(range(first, first + held)), couple is not None
    vmem = pl.BlockSpec(memory_space=pltpu.VMEM)
    operands = [mat, *blocks] + ([acc] if acc is not None else []) + ([couple] if finish else [])
    out_shape = jax.ShapeDtypeStruct((pairs, HALF if finish else 2 * HALF, width), jnp.bfloat16 if finish else jnp.float32)
    flops = 2 * pairs * 2 * HALF * width * (len(slots) * HALF + (width // 2 if finish else 0))
    return pl.pallas_call(
        functools.partial(sum_kernel, pairs, slots, len(blocks), acc is not None, finish),
        out_shape=out_shape,
        in_specs=[vmem] * len(operands),
        out_specs=vmem,
        scratch_shapes=[pltpu.VMEM((len(slots) * HALF, width), blocks[0].dtype)],
        compiler_params=pltpu.CompilerParams(vmem_limit_bytes=VMEM_LIMIT),
        cost_estimate=pl.CostEstimate(flops=flops, bytes_accessed=1 << 20, transcendentals=0),
        name=name,
    )(*operands)


def per_device(amps, fock, ladder, couple, tile_list):
    chips = lax.axis_size("virt") // 2
    total_tiles = fock.shape[1] // TILE
    pairs, _, nnz = tile_list.shape
    place = lax.axis_index("virt")
    chip, core = place // 2, place % 2

    hops = jnp.array([HOPS[abs(n)][0] * (-1 if n < 0 else 1) for n in ORDER], dtype=jnp.int32)
    other = jnp.array([HOPS[abs(n)][1] ^ (n < 0) for n in ORDER], dtype=jnp.int32)
    way = jnp.where(core == 0, -1, 1)
    half_of = jnp.where(other == 1, 1 - core, core)
    slot_tiles = ((chip + way * hops + chips) % chips * 2 * SPLIT + half_of * SPLIT).astype(jnp.int32)
    columns = jnp.arange(total_tiles, dtype=jnp.int32)
    masks = jnp.any(tile_list.reshape(pairs * SPLIT, nnz)[:, :, None] == columns, axis=1).astype(jnp.int32)

    x0 = amps
    x1, s1 = ring_step(x0), ring_step(x0, cross=1)
    mat = screened(slot_tiles, masks, fock, ladder, pairs)
    x2, s2 = ring_step(after(x1, mat)), ring_step(s1)
    acc = sum_slots("sum_1", mat, (x0, x1, s1), 0)
    x3, s3 = ring_step(after(x2, acc)), ring_step(s2)
    acc = sum_slots("sum_2", mat, (core_swap(x1), core_swap(s1), x2, s2), 3, acc)
    x4 = ring_step(after(x3, acc))
    acc = sum_slots("sum_3", mat, (core_swap(jnp.concatenate([x2, x0])), core_swap(s2), x3), 7, acc)
    acc = sum_slots("sum_4", mat, (core_swap(x3), core_swap(s3), s3, x4), 11, acc)
    x4_other = core_swap(x4)
    half_term = sum_slots("sum_5", mat, (x4_other,), 15, acc, couple)
    terms = [term.astype(jnp.float32) for term in (half_term, *mirror_swap(half_term))]
    return (terms[0] + (terms[1] + terms[2])).astype(jnp.bfloat16)


def solution(mesh):
    in_specs = (
        P("pair", "virt", None),
        P("virt", None),
        P("virt", None),
        P(),
        P("pair", "virt", None),
    )
    out_specs = P("pair", "virt", None)
    return jax.shard_map(
        per_device, mesh=mesh, in_specs=in_specs, out_specs=out_specs, check_vma=False
    )
```

```python
import functools

import jax
import jax.numpy as jnp
from jax import lax
from jax.experimental import pallas as pl
from jax.experimental.pallas import tpu as pltpu
from jax.sharding import PartitionSpec as P

TILE = 128
HALF = 256
SPLIT = HALF // TILE
VMEM_LIMIT = 24 * 1024 * 1024
RING = 16
HOPS = (None, (0, 0), (1, 0), (1, 1), (2, 0), (2, 1), (3, 0), (3, 1), (4, 0))
ORDER = (1, 2, 3, -2, -3, 4, 5, -4, -1, -5, 6, -6, -7, 7, 8, -8)


def core_swap(block):
    count = lax.axis_size("virt")
    return lax.ppermute(block, "virt", [(v, v ^ 1) for v in range(count)])


def ring_step(block, cross=0):
    chips = lax.axis_size("virt") // 2
    route = [(2 * c + cross, 2 * ((c + 1) % chips)) for c in range(chips)]
    route += [(2 * c + 1 - cross, 2 * ((c - 1) % chips) + 1) for c in range(chips)]
    return lax.ppermute(block, "virt", route)


def mirror_of(place, count):
    nbits = count.bit_length() - 1
    return count - 1 - sum(((place >> b) & 1) << (nbits - 1 - b) for b in range(nbits))


def detours(rows):
    moves = []
    for x, z in enumerate((3, 1, 2, 3)):
        for core in range(2):
            moves.append(((x, z), (x, RING // 2), core))
            moves.append(((rows - 1 - x, RING - 1 - z), (rows - 1 - x, RING // 2 - 1), core))
    for z, row in ((5, 1), (6, 2), (9, 1), (10, 2)):
        moves.append(((0, z), (row, z), 0))
        moves.append(((rows - 1, RING - 1 - z), (rows - 1 - row, RING - 1 - z), 1))
    return [(place[0] * RING + place[1], stop[0] * RING + stop[1], core) for place, stop, core in moves]


def mirror_swap(block):
    count, across = lax.axis_size("pair"), lax.axis_size("virt")
    axes = ("pair", "virt")
    first, second, direct = [], [], []
    moves = {(place, core): stop for place, stop, core in detours(count // RING)}
    for place in range(count):
        for v in range(across):
            here, end = place * across + v, mirror_of(place, count) * across + v
            if (place, v % 2) in moves:
                stop = moves[place, v % 2] * across + v
                first.append((here, stop))
                second.append((stop, end))
            else:
                direct.append((here, end))
    halfway = lax.ppermute(block, axes, first)
    straight = lax.ppermute(block, axes, direct)
    return straight, lax.ppermute(halfway, axes, second)


def after(block, *earlier):
    return lax.optimization_barrier((block, *earlier))[0]


def screen_kernel(pairs, slot_ref, mask_ref, fock, ladder, out_ref):
    for n in range(out_ref.shape[2] // HALF):
        for q in range(SPLIT):
            tile = slot_ref[n] + q
            columns = pl.ds(pl.multiple_of(tile * TILE, TILE), TILE)
            for r in range(SPLIT):
                keep = [mask_ref[p * SPLIT + r, tile] != 0 for p in range(pairs)]
                for i, mat in enumerate((fock, ladder)):
                    block = mat[r * TILE : (r + 1) * TILE, columns]
                    for p in range(pairs):
                        out_ref[
                            p,
                            i * HALF + r * TILE : i * HALF + (r + 1) * TILE,
                            n * HALF + q * TILE : n * HALF + (q + 1) * TILE,
                        ] = jnp.where(keep[p], block, jnp.zeros_like(block))


def screened(slot_tiles, masks, fock, ladder, pairs):
    smem = pl.BlockSpec(memory_space=pltpu.SMEM)
    vmem = pl.BlockSpec(memory_space=pltpu.VMEM)
    count, dtype = slot_tiles.shape[0], fock.dtype
    return pl.pallas_call(
        functools.partial(screen_kernel, pairs),
        out_shape=jax.ShapeDtypeStruct((pairs, 2 * HALF, count * HALF), dtype),
        in_specs=[smem, smem, vmem, vmem],
        out_specs=vmem,
        compiler_params=pltpu.CompilerParams(vmem_limit_bytes=VMEM_LIMIT),
        cost_estimate=pl.CostEstimate(flops=0, bytes_accessed=4 << 20, transcendentals=0),
        name="screened",
    )(slot_tiles, masks, fock, ladder)


def sum_kernel(pairs, slots, block_count, has_acc, finish, *refs):
    refs = list(refs)
    take = lambda n: [refs.pop(0) for _ in range(n)]
    mat, blocks = take(1)[0], take(block_count)
    acc_in = take(1)[0] if has_acc else None
    couple_ref = take(1)[0] if finish else None
    out, a_buf = refs
    lo, depth = slots[0] * HALF, len(slots) * HALF
    for p in range(pairs):
        held = [block.at[k + p] for block in blocks for k in range(0, block.shape[0], pairs)]
        for n, block in enumerate(held):
            a_buf[n * HALF : (n + 1) * HALF, :] = block[...]
        acc = jnp.dot(mat[p, :, lo : lo + depth], a_buf[...], preferred_element_type=jnp.float32)
        if has_acc:
            acc = acc_in[p] + acc
        if finish:
            lad = acc[HALF:, :].astype(jnp.bfloat16)
            acc = acc[:HALF, :] + jnp.dot(lad, couple_ref[...], preferred_element_type=jnp.float32)
        out[p] = acc.astype(out.dtype)


def sum_slots(name, mat, blocks, first, acc=None, couple=None):
    pairs, width = mat.shape[0], blocks[0].shape[2]
    held = sum(block.shape[0] for block in blocks) // pairs
    slots, finish = tuple(range(first, first + held)), couple is not None
    vmem = pl.BlockSpec(memory_space=pltpu.VMEM)
    operands = [mat, *blocks] + ([acc] if acc is not None else []) + ([couple] if finish else [])
    out_shape = jax.ShapeDtypeStruct((pairs, HALF if finish else 2 * HALF, width), jnp.bfloat16 if finish else jnp.float32)
    flops = 2 * pairs * 2 * HALF * width * (len(slots) * HALF + (width // 2 if finish else 0))
    return pl.pallas_call(
        functools.partial(sum_kernel, pairs, slots, len(blocks), acc is not None, finish),
        out_shape=out_shape,
        in_specs=[vmem] * len(operands),
        out_specs=vmem,
        scratch_shapes=[pltpu.VMEM((len(slots) * HALF, width), blocks[0].dtype)],
        compiler_params=pltpu.CompilerParams(vmem_limit_bytes=VMEM_LIMIT),
        cost_estimate=pl.CostEstimate(flops=flops, bytes_accessed=1 << 20, transcendentals=0),
        name=name,
    )(*operands)


def per_device(amps, fock, ladder, couple, tile_list):
    chips = lax.axis_size("virt") // 2
    total_tiles = fock.shape[1] // TILE
    pairs, _, nnz = tile_list.shape
    place = lax.axis_index("virt")
    chip, core = place // 2, place % 2

    hops = jnp.array([HOPS[abs(n)][0] * (-1 if n < 0 else 1) for n in ORDER], dtype=jnp.int32)
    other = jnp.array([HOPS[abs(n)][1] ^ (n < 0) for n in ORDER], dtype=jnp.int32)
    way = jnp.where(core == 0, -1, 1)
    half_of = jnp.where(other == 1, 1 - core, core)
    slot_tiles = ((chip + way * hops + chips) % chips * 2 * SPLIT + half_of * SPLIT).astype(jnp.int32)
    columns = jnp.arange(total_tiles, dtype=jnp.int32)
    masks = jnp.any(tile_list.reshape(pairs * SPLIT, nnz)[:, :, None] == columns, axis=1).astype(jnp.int32)

    x0 = amps
    x1, s1 = ring_step(x0), ring_step(x0, cross=1)
    mat = screened(slot_tiles, masks, fock, ladder, pairs)
    x2, s2 = ring_step(after(x1, mat)), ring_step(s1)
    x3, s3 = ring_step(x2), ring_step(s2)
    acc = sum_slots("sum_1", mat, (x0, x1, s1, core_swap(x1), core_swap(s1), x2, s2), 0)
    x4 = ring_step(after(x3, acc))
    early = (core_swap(jnp.concatenate([x2, x0])), core_swap(s2), x3)
    acc = sum_slots("sum_3", mat, (*early, core_swap(x3), core_swap(s3), s3, x4), 7, acc)
    x4_other = core_swap(x4)
    half_term = sum_slots("sum_5", mat, (x4_other,), 15, acc, couple)
    terms = [term.astype(jnp.float32) for term in (half_term, *mirror_swap(half_term))]
    return (terms[0] + (terms[1] + terms[2])).astype(jnp.bfloat16)


def solution(mesh):
    in_specs = (
        P("pair", "virt", None),
        P("virt", None),
        P("virt", None),
        P(),
        P("pair", "virt", None),
    )
    out_specs = P("pair", "virt", None)
    return jax.shard_map(
        per_device, mesh=mesh, in_specs=in_specs, out_specs=out_specs, check_vma=False
    )
```
